32 devices in a mesh: rows: 8 (over z, y), cols: 4 (over x, core).
Axes of the slice: x: 2, y: 2, z: 4, core: 2. Of those that a mesh axis runs over, the one named last changes fastest.
Arguments:
- right_vecs: bfloat16 [2, 16384, 512], P(None, 'rows', 'cols'), may hold values from -6 to 6
- left_vecs: bfloat16 [2, 16384, 512], P(None, 'rows', 'cols'), may hold values from -0.0625 to 0.0625
- dip_blocks: bfloat16 [128, 8, 2, 128, 128], P('rows'), may hold values from -0.125 to 0.125
- block_cols: int32 [128, 8], P('rows'), may hold values from 0 to 127, as said below
- block_counts: int32 [128], P('rows'), may hold values from 1 to 8, as said below
Outputs:
- coupling: float32 [4, 128, 2, 512], P(None, 'rows')
The draws below stay inside these ranges and needn't reach their ends.
Inputs may be any that keep to these rules, and one draw needn't show every extreme that they name: Block row r's columns lie within 16 blocks of r: |block_cols[r, j] - r| <= 16, slots at or past block_counts[r] included; such slots are not used. Slots in use fill the first block_counts[r] slots of a block row.
All inputs are finite; a program needn't handle non-finite values.
Results may differ from the reference program's by a relative error of at most 0.0029.
Values may be sent and summed in bfloat16 or wider, within the bound.
A program may use at most 128 MiB of HBM per device.

```python
import jax
import jax.numpy as jnp
from jax import lax

K = 512
BS = 128
MAXB = 8
BPD = 16
NBR = 128
NR = 16384
KG = 128


def draw_block_cols(key, part):
    row_ids = jnp.arange(NBR, dtype=jnp.int32)
    offsets = jax.random.randint(key, (NBR, MAXB), -BPD, BPD + 1, dtype=jnp.int32)
    return jnp.clip(row_ids[:, None] + offsets, 0, NBR - 1).astype(jnp.int32)


def draw_block_counts(key, part):
    key_heavy, key_pick, key_high, key_low = jax.random.split(jax.random.fold_in(key, 7), 4)
    groups = NBR // BPD
    heavy = jax.random.randint(key_heavy, (groups,), 0, 4, dtype=jnp.int32) == 0
    chosen = jax.random.randint(key_pick, (), 0, groups, dtype=jnp.int32)
    heavy = heavy.at[chosen].set(True)
    heavy_rows = jnp.repeat(heavy, BPD)
    high = jax.random.randint(key_high, (NBR,), MAXB // 2, MAXB + 1, dtype=jnp.int32)
    low = jax.random.randint(key_low, (NBR,), 1, 3, dtype=jnp.int32)
    counts = jnp.where(heavy_rows, high, low)
    return counts.at[chosen * BPD].set(MAXB).astype(jnp.int32)


def raised(drawn, own_key, source, target, parts, factor):
    owner, partner = [(jnp.arange(drawn.shape[position]) // (drawn.shape[position] // parts)).reshape([-1 if axis == position else 1 for axis in range(drawn.ndim)]) for position in (source, target)]
    chosen = jax.random.permutation(own_key, parts)[partner]
    strong = (owner == chosen) | (owner == (partner + parts // 2) % parts)
    return jnp.where(strong, factor * drawn, drawn)


def block_levels(stream_key, shape, cuts, low, high):
    def one(axis_at, parts):
        steps = jax.random.uniform(jax.random.fold_in(jax.random.fold_in(stream_key, 6), axis_at), (parts,), jnp.float32, low / len(cuts), high / len(cuts))
        return jnp.repeat(jnp.exp(steps), shape[axis_at] // parts).reshape((-1,) + (1,) * (len(shape) - axis_at - 1))

    gain = one(*cuts[0])
    for cut in cuts[1:]:
        gain = gain * one(*cut)
    return gain


def normal_values(stream_key, dims, width, limit, shards=(), held_as=jnp.bfloat16):
    factor_of = block_levels(stream_key, dims, shards, -0.22, 0.18) if shards else 1.0
    array = jax.random.normal(stream_key, dims, jnp.float32) * width * factor_of
    return jnp.minimum(jnp.maximum(array, -limit), limit).astype(held_as)


def noise_with(own_key, dims, width, bound, cuts, heavy, held_as=jnp.bfloat16):
    entries = width * jax.random.normal(own_key, dims, jnp.float32)
    if cuts:
        entries = entries * block_levels(own_key, dims, cuts, -0.22, 0.18)
    return jnp.clip(raised(entries, jax.random.fold_in(own_key, 3), *heavy), -bound, bound).astype(held_as)


def setup_inputs(seed: int = 0) -> dict:
    key_of = jax.random.split(jax.random.key(seed), 6)
    return {
        "right_vecs": normal_values(key_of[0], (2, NR, K), 1.0, 6.0, ((1, 8), (2, 4))),
        "left_vecs": noise_with(key_of[1], (2, NR, K), NR ** -0.5, 0.0625, ((1, 8), (2, 4)), (1, 2, 8, 2.0)),
        "dip_blocks": normal_values(key_of[2], (NBR, MAXB, 2, BS, BS), (2 * MAXB * BS) ** -0.5, 0.125, ((0, 8),)),
        "block_cols": draw_block_cols(jax.random.fold_in(key_of[5], 71), 0),
        "block_counts": draw_block_counts(jax.random.fold_in(key_of[5], 71), 0),
    }


def reference(right_vecs, left_vecs, dip_blocks, block_cols, block_counts):
    blocked = right_vecs.reshape(2, NBR, BS, K)
    slot_ids = jnp.arange(MAXB, dtype=jnp.int32)

    def one_row(args):
        mats, cols, count = args
        vecs = jnp.take(blocked, cols, axis=1).astype(jnp.float32)
        valid = (slot_ids < count)[None, :, None, None]
        vecs = jnp.where(valid, vecs, jnp.zeros_like(vecs))
        mats = mats.astype(jnp.float32)
        real_part = jnp.einsum("jpq,jqk->pk", mats[:, 0], vecs[0]) - jnp.einsum("jpq,jqk->pk", mats[:, 1], vecs[1])
        imag_part = jnp.einsum("jpq,jqk->pk", mats[:, 0], vecs[1]) + jnp.einsum("jpq,jqk->pk", mats[:, 1], vecs[0])
        return jnp.stack([real_part, imag_part]).astype(jnp.bfloat16)

    rows_out = lax.map(one_row, (dip_blocks, block_cols, block_counts))
    image = jnp.transpose(rows_out, (1, 0, 2, 3)).reshape(2, NR, K)
    left_re = left_vecs[0].T
    left_im = left_vecs[1].T
    real_part = jnp.dot(left_re, image[0], preferred_element_type=jnp.float32) + jnp.dot(left_im, image[1], preferred_element_type=jnp.float32)
    imag_part = jnp.dot(left_re, image[1], preferred_element_type=jnp.float32) - jnp.dot(left_im, image[0], preferred_element_type=jnp.float32)
    return jnp.stack([real_part, imag_part], axis=1).reshape(K // KG, KG, 2, K)
```

```python
import functools

import jax
import jax.numpy as jnp
from jax import lax
from jax.experimental import pallas as pl
from jax.experimental.pallas import tpu as pltpu
from jax.sharding import PartitionSpec as P

MESH = pl.DeviceIdType.MESH
CHUNKS = 8


def remote(src, dst, send_sem, recv_sem, **device):
    return pltpu.make_async_remote_copy(
        src_ref=src,
        dst_ref=dst,
        send_sem=send_sem,
        recv_sem=recv_sem,
        device_id=device,
        device_id_type=MESH,
    )


def kernel(
    n, groups, reduce_inside,
    cols_ref, counts_ref, right_ref, left_ref, dip_ref, out_ref,
    vecs, left_own, left_all, dip, image, part, landed, final,
    near_send, near_recv, far_send, far_recv, across_send, across_recv,
    mate_send, mate_recv, pass_send, pass_recv,
    local_sem, left_sem, share_send, share_recv, final_send, final_recv,
):
    me = lax.axis_index("rows")
    col = lax.axis_index("cols")
    blocks = right_ref.shape[1]
    slots = dip_ref.shape[1]
    size = right_ref.shape[2]
    width = right_ref.shape[3]
    span = blocks * size
    step_blocks = blocks // CHUNKS
    step_rows = span // CHUNKS

    parity = lax.rem(me, 2)
    partner = me + 1 - 2 * parity
    ahead = me + 2 - 4 * parity
    behind = me - 2 + 4 * parity
    near_off = 2 * blocks * (1 - parity)
    far_off = 2 * blocks * parity
    has_ahead = jnp.logical_and(ahead >= 0, ahead < n)
    has_behind = jnp.logical_and(behind >= 0, behind < n)
    mate = col + 1 - 2 * lax.rem(col, 2)
    across = lax.rem(col + 2, groups)

    own_left = pltpu.make_async_copy(left_ref, left_own, left_sem)
    own_left.start()

    barrier = pltpu.get_barrier_semaphore()
    if reduce_inside:
        for d in range(1, n):
            pl.semaphore_signal(barrier, inc=1, device_id={"rows": lax.rem(me + d, n)}, device_id_type=MESH)
        for d in range(1, groups):
            pl.semaphore_signal(barrier, inc=1, device_id={"cols": lax.rem(col + d, groups)}, device_id_type=MESH)
        pl.semaphore_wait(barrier, n - 1 + groups - 1)
    else:
        pl.semaphore_signal(barrier, inc=1, device_id={"rows": partner}, device_id_type=MESH)
        pl.semaphore_signal(barrier, inc=1, device_id={"cols": mate}, device_id_type=MESH)
        pl.semaphore_signal(barrier, inc=1, device_id={"cols": across}, device_id_type=MESH)

        @pl.when(has_ahead)
        def _():
            pl.semaphore_signal(barrier, inc=1, device_id={"rows": ahead}, device_id_type=MESH)

        @pl.when(has_behind)
        def _():
            pl.semaphore_signal(barrier, inc=1, device_id={"rows": behind}, device_id_type=MESH)

        pl.semaphore_wait(barrier, 3 + has_ahead.astype(jnp.int32) + has_behind.astype(jnp.int32))

    def near(k):
        return remote(
            right_ref.at[:, pl.ds(k * step_blocks, step_blocks)],
            vecs.at[:, pl.ds(far_off + k * step_blocks, step_blocks)],
            near_send.at[k], near_recv.at[k], rows=partner,
        )

    def far(k):
        return remote(
            vecs.at[:, pl.ds(near_off + k * step_blocks, step_blocks)],
            vecs.at[:, pl.ds(far_off + k * step_blocks, step_blocks)],
            far_send.at[k], far_recv.at[k], rows=ahead,
        )

    def to_across(k):
        return remote(left_all.at[col, k], left_all.at[col, k], across_send.at[k], across_recv.at[k], cols=across)

    def to_mate(k):
        return remote(left_all.at[col, k], left_all.at[col, k], mate_send.at[k], mate_recv.at[k], cols=mate)

    def passed(k):
        return remote(left_all.at[across, k], left_all.at[across, k], pass_send.at[k], pass_recv.at[k], cols=mate)

    for k in range(CHUNKS):
        near(k).start()
    own_left.wait()
    for k in range(CHUNKS):
        for c in range(2):
            left_all[col, k, c * width:(c + 1) * width, :] = left_own[c, k * step_rows:(k + 1) * step_rows, :].T
        to_across(k).start()
        to_mate(k).start()
    own_vecs = pltpu.make_async_copy(right_ref, vecs.at[:, pl.ds(blocks, blocks)], local_sem.at[0])
    own_vecs.start()
    own_dip = pltpu.make_async_copy(dip_ref, dip, local_sem.at[1])
    own_dip.start()
    for k in range(CHUNKS):
        near(k).wait_recv()

        @pl.when(has_ahead)
        def _():
            far(k).start()

        to_across(k).wait_recv()
        passed(k).start()
    own_vecs.wait()
    own_dip.wait()
    for k in range(CHUNKS):

        @pl.when(has_behind)
        def _():
            far(k).wait_recv()

    first = (me - 1) * blocks

    def block_row(i, carry):
        count = counts_ref[i]
        total = jnp.zeros((size, 2 * width), jnp.float32)
        for j in range(slots):
            at = jnp.clip(cols_ref[i, j] - first, 0, 3 * blocks - 1)
            real = vecs[0, at]
            imag = vecs[1, at]
            rhs = jnp.concatenate(
                [jnp.concatenate([real, imag], axis=1), jnp.concatenate([-imag, real], axis=1)], axis=0
            )
            lhs = jnp.concatenate([dip[i, j, 0], dip[i, j, 1]], axis=1)
            lhs = jnp.where(j < count, lhs, jnp.zeros_like(lhs))
            total = total + jnp.dot(lhs, rhs, preferred_element_type=jnp.float32)
        image[pl.ds(i * size, size), :] = total.astype(image.dtype)
        return carry

    lax.fori_loop(0, blocks, block_row, 0)

    for k in range(CHUNKS):
        to_mate(k).wait_recv()
        passed(k).wait_recv()

    def product(g):
        total = jnp.zeros((2 * width, 2 * width), jnp.float32)
        for k in range(CHUNKS):
            total = total + jnp.dot(
                left_all[g, k], image[k * step_rows:(k + 1) * step_rows, :], preferred_element_type=jnp.float32
            )
        real_part = total[:width, :width] + total[width:, width:]
        imag_part = total[:width, width:] - total[width:, :width]
        return real_part, imag_part

    if not reduce_inside:
        for g in range(groups):
            real_part, imag_part = product(g)
            out_ref[g, 0] = real_part
            out_ref[g, 1] = imag_part
    else:
        share = width // n
        for g in range(groups):
            real_part, imag_part = product(g)
            part[:, g, 0] = real_part.astype(part.dtype).reshape(n, share, width)
            part[:, g, 1] = imag_part.astype(part.dtype).reshape(n, share, width)

        def give(d):
            peer = lax.rem(me + d, n)
            return remote(part.at[peer], landed.at[me], share_send.at[peer], share_recv.at[me], rows=peer)

        def take(d):
            peer = lax.rem(me + d, n)
            return remote(part.at[peer], landed.at[peer], share_send.at[peer], share_recv.at[peer], rows=peer)

        for d in range(1, n):
            give(d).start()
        total = part[me].astype(jnp.float32)
        for d in range(1, n):
            take(d).wait_recv()
            total = total + landed[lax.rem(me + d, n)].astype(jnp.float32)
        final[col] = total

        def spread(d):
            peer = lax.rem(col + d, groups)
            return remote(final.at[col], final.at[col], final_send.at[d], final_recv.at[col], cols=peer)

        def gather(d):
            peer = lax.rem(col + d, groups)
            return remote(final.at[peer], final.at[peer], final_send.at[d], final_recv.at[peer], cols=peer)

        for d in range(1, groups):
            spread(d).start()
        for d in range(1, groups):
            gather(d).wait_recv()
        for c in range(groups):
            out_ref[:, :, :, c * width:(c + 1) * width] = final[c]
        for d in range(1, n):
            give(d).wait_send()
        for d in range(1, groups):
            spread(d).wait_send()

    for k in range(CHUNKS):
        near(k).wait_send()

        @pl.when(has_ahead)
        def _():
            far(k).wait_send()

        to_across(k).wait_send()
        to_mate(k).wait_send()
        passed(k).wait_send()


def local(n, groups, right_vecs, left_vecs, dip_blocks, block_cols, block_counts):
    span, width = right_vecs.shape[1:]
    blocks, slots, _, size, _ = dip_blocks.shape
    share = width // n
    reduce_inside = share % 16 == 0
    right = right_vecs.reshape(2, blocks, size, width)
    if reduce_inside:
        out_shape = (groups, 2, share, groups * width)
        part_shape = (n, groups, 2, share, width)
        final_shape = (groups, groups, 2, share, width)
    else:
        out_shape = (groups, 2, width, width)
        part_shape = final_shape = (1, 1, 1, 16, 128)
    dma = pltpu.SemaphoreType.DMA
    result = pl.pallas_call(
        functools.partial(kernel, n, groups, reduce_inside),
        out_shape=jax.ShapeDtypeStruct(out_shape, jnp.float32),
        in_specs=[pl.BlockSpec(memory_space=pltpu.SMEM)] * 2 + [pl.BlockSpec(memory_space=pl.ANY)] * 3,
        out_specs=pl.BlockSpec(memory_space=pltpu.VMEM),
        scratch_shapes=[
            pltpu.VMEM((2, 3 * blocks, size, width), jnp.bfloat16),
            pltpu.VMEM((2, span, width), jnp.bfloat16),
            pltpu.VMEM((groups, CHUNKS, 2 * width, span // CHUNKS), jnp.bfloat16),
            pltpu.VMEM(dip_blocks.shape, jnp.bfloat16),
            pltpu.VMEM((span, 2 * width), jnp.bfloat16),
            pltpu.VMEM(part_shape, jnp.bfloat16),
            pltpu.VMEM(part_shape, jnp.bfloat16),
            pltpu.VMEM(final_shape, jnp.float32),
        ] + [dma((CHUNKS,))] * 10 + [
            dma((2,)), dma, dma((n,)), dma((n,)), dma((groups,)), dma((groups,)),
        ],
        compiler_params=pltpu.CompilerParams(
            collective_id=0, has_side_effects=True, vmem_limit_bytes=40 * 1024 * 1024
        ),
    )(block_cols, block_counts, right, left_vecs, dip_blocks)
    if reduce_inside:
        return jnp.transpose(result, (0, 2, 1, 3))
    shares = lax.psum_scatter(jnp.transpose(result, (0, 2, 1, 3)), "rows", scatter_dimension=1, tiled=True)
    return lax.all_gather(shares, "cols", axis=3, tiled=True)


def solution(mesh):
    in_specs = (
        P(None, "rows", "cols"),
        P(None, "rows", "cols"),
        P("rows", None, None, None, None),
        P("rows", None),
        P("rows"),
    )
    out_specs = P(None, "rows", None, None)
    body = functools.partial(local, mesh.shape["rows"], mesh.shape["cols"])
    return jax.shard_map(body, mesh=mesh, in_specs=in_specs, out_specs=out_specs, check_vma=False)
```

```python
import functools

import jax
import jax.numpy as jnp
from jax import lax
from jax.experimental import pallas as pl
from jax.experimental.pallas import tpu as pltpu
from jax.sharding import PartitionSpec as P

MESH = pl.DeviceIdType.MESH
CHUNKS = 16
LEFT_CHUNKS = 8
HALVES = 2


def remote(src, dst, send_sem, recv_sem, **device):
    return pltpu.make_async_remote_copy(
        src_ref=src,
        dst_ref=dst,
        send_sem=send_sem,
        recv_sem=recv_sem,
        device_id=device,
        device_id_type=MESH,
    )


def kernel(
    n, groups, reduce_inside,
    cols_ref, counts_ref, right_ref, left_ref, dip_ref, out_ref,
    vecs, left_own, left_all, dip, pairs, mats, image, part, landed, final,
    near_send, near_recv, far_send, far_recv, across_send, across_recv,
    mate_send, mate_recv, pass_send, pass_recv,
    local_sem, left_sem, share_send, share_recv, final_send, final_recv,
):
    me = lax.axis_index("rows")
    col = lax.axis_index("cols")
    blocks = right_ref.shape[1]
    slots = dip_ref.shape[1]
    size = right_ref.shape[2]
    width = right_ref.shape[3]
    span = blocks * size
    step_blocks = blocks // CHUNKS
    step_rows = span // LEFT_CHUNKS

    parity = lax.rem(me, 2)
    partner = me + 1 - 2 * parity
    ahead = me + 2 - 4 * parity
    behind = me - 2 + 4 * parity
    near_off = 2 * blocks * (1 - parity)
    far_off = 2 * blocks * parity
    has_ahead = jnp.logical_and(ahead >= 0, ahead < n)
    has_behind = jnp.logical_and(behind >= 0, behind < n)
    mate = col + 1 - 2 * lax.rem(col, 2)
    across = lax.rem(col + 2, groups)

    own_left = pltpu.make_async_copy(left_ref, left_own, left_sem)
    own_left.start()
    own_vecs = pltpu.make_async_copy(right_ref, vecs.at[:, pl.ds(blocks, blocks)], local_sem.at[0])
    own_dip = pltpu.make_async_copy(dip_ref, dip, local_sem.at[1])

    barrier = pltpu.get_barrier_semaphore()
    if reduce_inside:
        for d in range(1, n):
            pl.semaphore_signal(barrier, inc=1, device_id={"rows": lax.rem(me + d, n)}, device_id_type=MESH)
        for d in range(1, groups):
            pl.semaphore_signal(barrier, inc=1, device_id={"cols": lax.rem(col + d, groups)}, device_id_type=MESH)
        pl.semaphore_wait(barrier, n - 1 + groups - 1)
    else:
        pl.semaphore_signal(barrier, inc=1, device_id={"rows": partner}, device_id_type=MESH)
        pl.semaphore_signal(barrier, inc=1, device_id={"cols": mate}, device_id_type=MESH)
        pl.semaphore_signal(barrier, inc=1, device_id={"cols": across}, device_id_type=MESH)

        @pl.when(has_ahead)
        def _():
            pl.semaphore_signal(barrier, inc=1, device_id={"rows": ahead}, device_id_type=MESH)

        @pl.when(has_behind)
        def _():
            pl.semaphore_signal(barrier, inc=1, device_id={"rows": behind}, device_id_type=MESH)

        pl.semaphore_wait(barrier, 3 + has_ahead.astype(jnp.int32) + has_behind.astype(jnp.int32))

    def near(k):
        return remote(
            right_ref.at[:, pl.ds(k * step_blocks, step_blocks)],
            vecs.at[:, pl.ds(far_off + k * step_blocks, step_blocks)],
            near_send.at[k], near_recv.at[k], rows=partner,
        )

    def far(k):
        return remote(
            vecs.at[:, pl.ds(near_off + k * step_blocks, step_blocks)],
            vecs.at[:, pl.ds(far_off + k * step_blocks, step_blocks)],
            far_send.at[k], far_recv.at[k], rows=ahead,
        )

    def to_across(k):
        return remote(left_all.at[col, k], left_all.at[col, k], across_send.at[k], across_recv.at[k], cols=across)

    def to_mate(k):
        return remote(left_all.at[col, k], left_all.at[col, k], mate_send.at[k], mate_recv.at[k], cols=mate)

    def passed(k):
        return remote(left_all.at[across, k], left_all.at[across, k], pass_send.at[k], pass_recv.at[k], cols=mate)

    for k in range(CHUNKS):
        near(k).start()
    own_left.wait()
    for k in range(LEFT_CHUNKS):
        for c in range(2):
            left_all[col, k, c * width:(c + 1) * width, :] = left_own[c, k * step_rows:(k + 1) * step_rows, :].T
        to_across(k).start()
        to_mate(k).start()
    own_vecs.start()
    own_dip.start()

    def pair(at):
        real = vecs[0, at]
        imag = vecs[1, at]
        pairs[at, :size, :width] = real
        pairs[at, :size, width:] = imag
        pairs[at, size:, :width] = -imag
        pairs[at, size:, width:] = real

    def lay_out(i, carry):
        count = counts_ref[i]
        for j in range(slots):
            for c in range(2):
                block = dip[i, j, c]
                at = (2 * j + c) * size
                mats[i, :, at:at + size] = jnp.where(j < count, block, jnp.zeros_like(block))
        return carry

    def far_pairs(k):
        @pl.when(has_behind)
        def _():
            far(k).wait_recv()

        for b in range(step_blocks):
            pair(far_off + k * step_blocks + b)

    lag = 2
    half_way = CHUNKS // 2
    every = CHUNKS // LEFT_CHUNKS
    per_step = blocks // half_way
    for k in range(CHUNKS):
        near(k).wait_recv()

        @pl.when(has_ahead)
        def _():
            far(k).start()

        if k % every == every - 1:
            to_across(k // every).wait_recv()
            passed(k // every).start()
        for b in range(step_blocks):
            pair(near_off + k * step_blocks + b)
        if k < half_way:
            if k == 0:
                own_vecs.wait()
            for b in range(per_step):
                pair(blocks + k * per_step + b)
        else:
            if k == half_way:
                own_dip.wait()
            start = (k - half_way) * per_step
            lax.fori_loop(start, start + per_step, lay_out, 0)
        if k >= lag:
            far_pairs(k - lag)
    for k in range(CHUNKS - lag, CHUNKS):
        far_pairs(k)

    first = (me - 1) * blocks

    def block_row(i, carry):
        total = jnp.zeros((size, 2 * width), jnp.float32)
        for j in range(slots):
            at = jnp.clip(cols_ref[j, i] - first, 0, 3 * blocks - 1)
            lhs = mats[i, :, 2 * j * size:2 * (j + 1) * size]
            total = total + jnp.dot(lhs, pairs[at], preferred_element_type=jnp.float32)
        image[pl.ds(i * size, size), :] = total.astype(image.dtype)
        return carry

    lax.fori_loop(0, blocks, block_row, 0)

    for k in range(LEFT_CHUNKS):
        to_mate(k).wait_recv()
        passed(k).wait_recv()

    def product(g):
        total = jnp.zeros((2 * width, 2 * width), jnp.float32)
        for k in range(LEFT_CHUNKS):
            total = total + jnp.dot(
                left_all[g, k], image[k * step_rows:(k + 1) * step_rows, :], preferred_element_type=jnp.float32
            )
        real_part = total[:width, :width] + total[width:, width:]
        imag_part = total[:width, width:] - total[width:, :width]
        return real_part, imag_part

    if not reduce_inside:
        for g in range(groups):
            real_part, imag_part = product(g)
            out_ref[g, 0] = real_part
            out_ref[g, 1] = imag_part
    else:
        share = width // n
        half = groups // HALVES
        order = sorted(range(1, n), key=lambda d: abs(d - n // 2))

        def give(h, d):
            peer = lax.rem(me + d, n)
            return remote(part.at[h, peer], landed.at[h, me], share_send.at[h, peer], share_recv.at[h, me], rows=peer)

        def take(h, d):
            peer = lax.rem(me + d, n)
            return remote(part.at[h, peer], landed.at[h, peer], share_send.at[h, peer], share_recv.at[h, peer], rows=peer)

        def spread(h, d):
            peer = lax.rem(col + d, groups)
            return remote(final.at[h, col], final.at[h, col], final_send.at[h, d], final_recv.at[h, col], cols=peer)

        def gather(h, d):
            peer = lax.rem(col + d, groups)
            return remote(final.at[h, peer], final.at[h, peer], final_send.at[h, d], final_recv.at[h, peer], cols=peer)

        for h in range(HALVES):
            for g in range(half):
                real_part, imag_part = product(h * half + g)
                part[h, :, g, 0] = real_part.astype(part.dtype).reshape(n, share, width)
                part[h, :, g, 1] = imag_part.astype(part.dtype).reshape(n, share, width)
            for d in order:
                give(h, d).start()
        for h in range(HALVES):
            total = part[h, me].astype(jnp.float32)
            for d in order[::-1]:
                take(h, d).wait_recv()
                total = total + landed[h, lax.rem(me + d, n)].astype(jnp.float32)
            final[h, col] = total
            for d in (2, 3, 1):
                spread(h, d).start()
        for h in range(HALVES):
            for d in range(1, groups):
                gather(h, d).wait_recv()
            for c in range(groups):
                for part_at in range(2):
                    out_ref[h * half:(h + 1) * half, :, part_at, c * width:(c + 1) * width] = final[h, c, :, part_at]
        for h in range(HALVES):
            for d in order:
                give(h, d).wait_send()
            for d in range(1, groups):
                spread(h, d).wait_send()

    for k in range(CHUNKS):
        near(k).wait_send()

        @pl.when(has_ahead)
        def _():
            far(k).wait_send()

    for k in range(LEFT_CHUNKS):
        to_across(k).wait_send()
        to_mate(k).wait_send()
        passed(k).wait_send()


def local(n, groups, right_vecs, left_vecs, dip_blocks, block_cols, block_counts):
    span, width = right_vecs.shape[1:]
    blocks, slots, _, size, _ = dip_blocks.shape
    share = width // n
    reduce_inside = share % 16 == 0
    right = right_vecs.reshape(2, blocks, size, width)
    if reduce_inside:
        half = groups // HALVES
        out_shape = (groups, share, 2, groups * width)
        part_shape = (HALVES, n, half, 2, share, width)
        final_shape = (HALVES, groups, half, 2, share, width)
    else:
        out_shape = (groups, 2, width, width)
        part_shape = final_shape = (1, 1, 1, 16, 128)
    dma = pltpu.SemaphoreType.DMA
    result = pl.pallas_call(
        functools.partial(kernel, n, groups, reduce_inside),
        out_shape=jax.ShapeDtypeStruct(out_shape, jnp.float32),
        in_specs=[pl.BlockSpec(memory_space=pltpu.SMEM)] * 2 + [pl.BlockSpec(memory_space=pl.ANY)] * 3,
        out_specs=pl.BlockSpec(memory_space=pltpu.VMEM),
        scratch_shapes=[
            pltpu.VMEM((2, 3 * blocks, size, width), jnp.bfloat16),
            pltpu.VMEM((2, span, width), jnp.bfloat16),
            pltpu.VMEM((groups, LEFT_CHUNKS, 2 * width, span // LEFT_CHUNKS), jnp.bfloat16),
            pltpu.VMEM(dip_blocks.shape, jnp.bfloat16),
            pltpu.VMEM((3 * blocks, 2 * size, 2 * width), jnp.bfloat16),
            pltpu.VMEM((blocks, size, 2 * slots * size), jnp.bfloat16),
            pltpu.VMEM((span, 2 * width), jnp.bfloat16),
            pltpu.VMEM(part_shape, jnp.bfloat16),
            pltpu.VMEM(part_shape, jnp.bfloat16),
            pltpu.VMEM(final_shape, jnp.float32),
        ] + [dma((CHUNKS,))] * 4 + [dma((LEFT_CHUNKS,))] * 6 + [
            dma((2,)), dma, dma((HALVES, n)), dma((HALVES, n)), dma((HALVES, groups)), dma((HALVES, groups)),
        ],
        compiler_params=pltpu.CompilerParams(
            collective_id=0, has_side_effects=True, vmem_limit_bytes=60 * 1024 * 1024
        ),
    )(block_cols.T, block_counts, right, left_vecs, dip_blocks)
    if reduce_inside:
        return result
    shares = lax.psum_scatter(jnp.transpose(result, (0, 2, 1, 3)), "rows", scatter_dimension=1, tiled=True)
    return lax.all_gather(shares, "cols", axis=3, tiled=True)


def solution(mesh):
    in_specs = (
        P(None, "rows", "cols"),
        P(None, "rows", "cols"),
        P("rows", None, None, None, None),
        P("rows", None),
        P("rows"),
    )
    out_specs = P(None, "rows", None, None)
    body = functools.partial(local, mesh.shape["rows"], mesh.shape["cols"])
    return jax.shard_map(body, mesh=mesh, in_specs=in_specs, out_specs=out_specs, check_vma=False)
```

```python
import functools

import jax
import jax.numpy as jnp
from jax import lax
from jax.experimental import pallas as pl
from jax.experimental.pallas import tpu as pltpu
from jax.sharding import PartitionSpec as P

MESH = pl.DeviceIdType.MESH
CHUNKS = 16
LEFT_CHUNKS = 8
HALVES = 2


def remote(src, dst, send_sem, recv_sem, **device):
    return pltpu.make_async_remote_copy(
        src_ref=src,
        dst_ref=dst,
        send_sem=send_sem,
        recv_sem=recv_sem,
        device_id=device,
        device_id_type=MESH,
    )


def kernel(
    n, groups, reduce_inside,
    cols_ref, counts_ref, right_ref, left_ref, dip_ref, out_ref,
    vecs, left_own, left_all, dip, pairs, mats, image, part, landed, final,
    near_send, near_recv, far_send, far_recv, across_send, across_recv,
    mate_send, mate_recv, pass_send, pass_recv,
    local_sem, left_sem, share_send, share_recv, final_send, final_recv,
):
    me = lax.axis_index("rows")
    col = lax.axis_index("cols")
    blocks = right_ref.shape[1]
    slots = dip_ref.shape[1]
    size = right_ref.shape[2]
    width = right_ref.shape[3]
    span = blocks * size
    step_blocks = blocks // CHUNKS
    step_rows = span // LEFT_CHUNKS

    parity = lax.rem(me, 2)
    partner = me + 1 - 2 * parity
    ahead = me + 2 - 4 * parity
    behind = me - 2 + 4 * parity
    near_off = 2 * blocks * (1 - parity)
    far_off = 2 * blocks * parity
    has_ahead = jnp.logical_and(ahead >= 0, ahead < n)
    has_behind = jnp.logical_and(behind >= 0, behind < n)
    mate = col + 1 - 2 * lax.rem(col, 2)
    across = lax.rem(col + 2, groups)

    own_left = pltpu.make_async_copy(left_ref, left_own, left_sem)
    own_left.start()
    own_vecs = pltpu.make_async_copy(right_ref, vecs.at[:, pl.ds(blocks, blocks)], local_sem.at[0])
    own_dip = pltpu.make_async_copy(dip_ref, dip, local_sem.at[1])

    barrier = pltpu.get_barrier_semaphore()
    if reduce_inside:
        for d in range(1, n):
            pl.semaphore_signal(barrier, inc=1, device_id={"rows": lax.rem(me + d, n)}, device_id_type=MESH)
        for d in range(1, groups):
            pl.semaphore_signal(barrier, inc=1, device_id={"cols": lax.rem(col + d, groups)}, device_id_type=MESH)
        pl.semaphore_wait(barrier, n - 1 + groups - 1)
    else:
        pl.semaphore_signal(barrier, inc=1, device_id={"rows": partner}, device_id_type=MESH)
        pl.semaphore_signal(barrier, inc=1, device_id={"cols": mate}, device_id_type=MESH)
        pl.semaphore_signal(barrier, inc=1, device_id={"cols": across}, device_id_type=MESH)

        @pl.when(has_ahead)
        def _():
            pl.semaphore_signal(barrier, inc=1, device_id={"rows": ahead}, device_id_type=MESH)

        @pl.when(has_behind)
        def _():
            pl.semaphore_signal(barrier, inc=1, device_id={"rows": behind}, device_id_type=MESH)

        pl.semaphore_wait(barrier, 3 + has_ahead.astype(jnp.int32) + has_behind.astype(jnp.int32))

    def got(k):
        return step_blocks * (k * parity + (CHUNKS - 1 - k) * (1 - parity))

    def sent(k):
        return step_blocks * (k * (1 - parity) + (CHUNKS - 1 - k) * parity)

    def near(k):
        return remote(
            right_ref.at[:, pl.ds(sent(k), step_blocks)],
            vecs.at[:, pl.ds(far_off + sent(k), step_blocks)],
            near_send.at[k], near_recv.at[k], rows=partner,
        )

    def far(k):
        return remote(
            vecs.at[:, pl.ds(near_off + got(k), step_blocks)],
            vecs.at[:, pl.ds(far_off + got(k), step_blocks)],
            far_send.at[k], far_recv.at[k], rows=ahead,
        )

    def to_across(k):
        return remote(left_all.at[col, k], left_all.at[col, k], across_send.at[k], across_recv.at[k], cols=across)

    def to_mate(k):
        return remote(left_all.at[col, k], left_all.at[col, k], mate_send.at[k], mate_recv.at[k], cols=mate)

    def passed(k):
        return remote(left_all.at[across, k], left_all.at[across, k], pass_send.at[k], pass_recv.at[k], cols=mate)

    for k in range(CHUNKS):
        near(k).start()
    own_left.wait()
    for k in range(LEFT_CHUNKS):
        for c in range(2):
            left_all[col, k, c * width:(c + 1) * width, :] = left_own[c, k * step_rows:(k + 1) * step_rows, :].T
        to_across(k).start()
        to_mate(k).start()
    own_vecs.start()
    own_dip.start()

    def pair(at):
        real = vecs[0, at]
        imag = vecs[1, at]
        pairs[at, :size, :width] = real
        pairs[at, :size, width:] = imag
        pairs[at, size:, :width] = -imag
        pairs[at, size:, width:] = real

    def lay_out(i, carry):
        count = counts_ref[i]
        for j in range(slots):
            for c in range(2):
                block = dip[i, j, c]
                at = (2 * j + c) * size
                mats[i, :, at:at + size] = jnp.where(j < count, block, jnp.zeros_like(block))
        return carry

    def far_pairs(k):
        @pl.when(has_behind)
        def _():
            far(k).wait_recv()

        for b in range(step_blocks):
            pair(far_off + got(k) + b)

    lag = CHUNKS // 4
    half_way = CHUNKS // 2
    every = CHUNKS // LEFT_CHUNKS
    per_step = blocks // half_way
    for k in range(CHUNKS):
        near(k).wait_recv()

        @pl.when(has_ahead)
        def _():
            far(k).start()

        if k % every == every - 1:
            to_across(k // every).wait_recv()
            passed(k // every).start()
        for b in range(step_blocks):
            pair(near_off + got(k) + b)
        if k < half_way:
            if k == 0:
                own_vecs.wait()
            for b in range(per_step):
                pair(blocks + k * per_step + b)
        else:
            if k == half_way:
                own_dip.wait()
            start = (k - half_way) * per_step
            lax.fori_loop(start, start + per_step, lay_out, 0)
        if k >= lag:
            far_pairs(k - lag)
    first = (me - 1) * blocks

    def block_row(at, carry):
        i = at * parity + (blocks - 1 - at) * (1 - parity)
        total = jnp.zeros((size, 2 * width), jnp.float32)
        for j in range(slots):
            source = jnp.clip(cols_ref[j, i] - first, 0, 3 * blocks - 1)
            lhs = mats[i, :, 2 * j * size:2 * (j + 1) * size]
            total = total + jnp.dot(lhs, pairs[source], preferred_element_type=jnp.float32)
        image[pl.ds(i * size, size), :] = total.astype(image.dtype)
        return carry

    ready = blocks - lag * step_blocks
    lax.fori_loop(0, ready, block_row, 0, unroll=4)
    for k in range(CHUNKS - lag, CHUNKS):
        far_pairs(k)
    lax.fori_loop(ready, blocks, block_row, 0, unroll=4)

    for k in range(LEFT_CHUNKS):
        to_mate(k).wait_recv()
        passed(k).wait_recv()

    def product(g):
        total = jnp.zeros((2 * width, 2 * width), jnp.float32)
        for k in range(LEFT_CHUNKS):
            total = total + jnp.dot(
                left_all[g, k], image[k * step_rows:(k + 1) * step_rows, :], preferred_element_type=jnp.float32
            )
        real_part = total[:width, :width] + total[width:, width:]
        imag_part = total[:width, width:] - total[width:, :width]
        return real_part, imag_part

    if not reduce_inside:
        for g in range(groups):
            real_part, imag_part = product(g)
            out_ref[g, 0] = real_part
            out_ref[g, 1] = imag_part
    else:
        share = width // n
        half = groups // HALVES
        order = sorted(range(1, n), key=lambda d: abs(d - n // 2))

        def give(h, d):
            peer = lax.rem(me + d, n)
            return remote(part.at[h, peer], landed.at[h, me], share_send.at[h, peer], share_recv.at[h, me], rows=peer)

        def take(h, d):
            peer = lax.rem(me + d, n)
            return remote(part.at[h, peer], landed.at[h, peer], share_send.at[h, peer], share_recv.at[h, peer], rows=peer)

        def spread(h, d):
            peer = lax.rem(col + d, groups)
            return remote(final.at[h, col], final.at[h, col], final_send.at[h, d], final_recv.at[h, col], cols=peer)

        def gather(h, d):
            peer = lax.rem(col + d, groups)
            return remote(final.at[h, peer], final.at[h, peer], final_send.at[h, d], final_recv.at[h, peer], cols=peer)

        for h in range(HALVES):
            for g in range(half):
                real_part, imag_part = product(h * half + g)
                part[h, :, g, 0] = real_part.astype(part.dtype).reshape(n, share, width)
                part[h, :, g, 1] = imag_part.astype(part.dtype).reshape(n, share, width)
            for d in order:
                give(h, d).start()
        for h in range(HALVES):
            total = part[h, me].astype(jnp.float32)
            for d in order[::-1]:
                take(h, d).wait_recv()
                total = total + landed[h, lax.rem(me + d, n)].astype(jnp.float32)
            final[h, col] = total
            for d in (2, 3, 1):
                spread(h, d).start()
        for h in range(HALVES):
            for d in range(1, groups):
                gather(h, d).wait_recv()
            for c in range(groups):
                for part_at in range(2):
                    out_ref[h * half:(h + 1) * half, :, part_at, c * width:(c + 1) * width] = final[h, c, :, part_at]
        for h in range(HALVES):
            for d in order:
                give(h, d).wait_send()
            for d in range(1, groups):
                spread(h, d).wait_send()

    for k in range(CHUNKS):
        near(k).wait_send()

        @pl.when(has_ahead)
        def _():
            far(k).wait_send()

    for k in range(LEFT_CHUNKS):
        to_across(k).wait_send()
        to_mate(k).wait_send()
        passed(k).wait_send()


def local(n, groups, right_vecs, left_vecs, dip_blocks, block_cols, block_counts):
    span, width = right_vecs.shape[1:]
    blocks, slots, _, size, _ = dip_blocks.shape
    share = width // n
    reduce_inside = share % 16 == 0
    right = right_vecs.reshape(2, blocks, size, width)
    if reduce_inside:
        half = groups // HALVES
        out_shape = (groups, share, 2, groups * width)
        part_shape = (HALVES, n, half, 2, share, width)
        final_shape = (HALVES, groups, half, 2, share, width)
    else:
        out_shape = (groups, 2, width, width)
        part_shape = final_shape = (1, 1, 1, 16, 128)
    dma = pltpu.SemaphoreType.DMA
    result = pl.pallas_call(
        functools.partial(kernel, n, groups, reduce_inside),
        out_shape=jax.ShapeDtypeStruct(out_shape, jnp.float32),
        in_specs=[pl.BlockSpec(memory_space=pltpu.SMEM)] * 2 + [pl.BlockSpec(memory_space=pl.ANY)] * 3,
        out_specs=pl.BlockSpec(memory_space=pltpu.VMEM),
        scratch_shapes=[
            pltpu.VMEM((2, 3 * blocks, size, width), jnp.bfloat16),
            pltpu.VMEM((2, span, width), jnp.bfloat16),
            pltpu.VMEM((groups, LEFT_CHUNKS, 2 * width, span // LEFT_CHUNKS), jnp.bfloat16),
            pltpu.VMEM(dip_blocks.shape, jnp.bfloat16),
            pltpu.VMEM((3 * blocks, 2 * size, 2 * width), jnp.bfloat16),
            pltpu.VMEM((blocks, size, 2 * slots * size), jnp.bfloat16),
            pltpu.VMEM((span, 2 * width), jnp.bfloat16),
            pltpu.VMEM(part_shape, jnp.bfloat16),
            pltpu.VMEM(part_shape, jnp.bfloat16),
            pltpu.VMEM(final_shape, jnp.float32),
        ] + [dma((CHUNKS,))] * 4 + [dma((LEFT_CHUNKS,))] * 6 + [
            dma((2,)), dma, dma((HALVES, n)), dma((HALVES, n)), dma((HALVES, groups)), dma((HALVES, groups)),
        ],
        compiler_params=pltpu.CompilerParams(
            collective_id=0, has_side_effects=True, vmem_limit_bytes=60 * 1024 * 1024
        ),
    )(block_cols.T, block_counts, right, left_vecs, dip_blocks)
    if reduce_inside:
        return result
    shares = lax.psum_scatter(jnp.transpose(result, (0, 2, 1, 3)), "rows", scatter_dimension=1, tiled=True)
    return lax.all_gather(shares, "cols", axis=3, tiled=True)


def solution(mesh):
    in_specs = (
        P(None, "rows", "cols"),
        P(None, "rows", "cols"),
        P("rows", None, None, None, None),
        P("rows", None),
        P("rows"),
    )
    out_specs = P(None, "rows", None, None)
    body = functools.partial(local, mesh.shape["rows"], mesh.shape["cols"])
    return jax.shard_map(body, mesh=mesh, in_specs=in_specs, out_specs=out_specs, check_vma=False)
```

```python
import functools

import jax
import jax.numpy as jnp
from jax import lax
from jax.experimental import pallas as pl
from jax.experimental.pallas import tpu as pltpu
from jax.sharding import PartitionSpec as P

MESH = pl.DeviceIdType.MESH
CHUNKS = 16
LEFT_CHUNKS = 8
HALVES = 2


def remote(src, dst, send_sem, recv_sem, **device):
    return pltpu.make_async_remote_copy(
        src_ref=src,
        dst_ref=dst,
        send_sem=send_sem,
        recv_sem=recv_sem,
        device_id=device,
        device_id_type=MESH,
    )


def kernel(
    n, groups, reduce_inside,
    cols_ref, counts_ref, right_ref, left_ref, dip_ref, out_ref,
    vecs, left_own, left_all, dip, pairs, mats, image, part, landed, final,
    near_send, near_recv, far_send, far_recv, across_send, across_recv,
    mate_send, mate_recv, pass_send, pass_recv,
    local_sem, left_sem, share_send, share_recv, final_send, final_recv, round_sem,
):
    me = lax.axis_index("rows")
    col = lax.axis_index("cols")
    blocks = right_ref.shape[1]
    slots = dip_ref.shape[1]
    size = right_ref.shape[2]
    width = right_ref.shape[3]
    span = blocks * size
    step_blocks = blocks // CHUNKS
    step_rows = span // LEFT_CHUNKS

    parity = lax.rem(me, 2)
    partner = me + 1 - 2 * parity
    ahead = me + 2 - 4 * parity
    behind = me - 2 + 4 * parity
    near_off = 2 * blocks * (1 - parity)
    far_off = 2 * blocks * parity
    has_ahead = jnp.logical_and(ahead >= 0, ahead < n)
    has_behind = jnp.logical_and(behind >= 0, behind < n)
    mate = col + 1 - 2 * lax.rem(col, 2)
    across = lax.rem(col + 2, groups)

    own_left = pltpu.make_async_copy(left_ref, left_own, left_sem)
    own_left.start()
    own_vecs = pltpu.make_async_copy(right_ref, vecs.at[:, pl.ds(blocks, blocks)], local_sem.at[0])
    own_dip = pltpu.make_async_copy(dip_ref, dip, local_sem.at[1])

    barrier = pltpu.get_barrier_semaphore()
    def greet(sem):
        pl.semaphore_signal(sem, inc=1, device_id={"rows": partner}, device_id_type=MESH)
        pl.semaphore_signal(sem, inc=1, device_id={"cols": mate}, device_id_type=MESH)
        pl.semaphore_signal(sem, inc=1, device_id={"cols": across}, device_id_type=MESH)

        @pl.when(has_ahead)
        def _():
            pl.semaphore_signal(sem, inc=1, device_id={"rows": ahead}, device_id_type=MESH)

        @pl.when(has_behind)
        def _():
            pl.semaphore_signal(sem, inc=1, device_id={"rows": behind}, device_id_type=MESH)

    neighbours = 3 + has_ahead.astype(jnp.int32) + has_behind.astype(jnp.int32)
    greet(barrier)
    pl.semaphore_wait(barrier, neighbours)

    def got(k):
        return step_blocks * (k * parity + (CHUNKS - 1 - k) * (1 - parity))

    def sent(k):
        return step_blocks * (k * (1 - parity) + (CHUNKS - 1 - k) * parity)

    def near(k):
        return remote(
            right_ref.at[:, pl.ds(sent(k), step_blocks)],
            vecs.at[:, pl.ds(far_off + sent(k), step_blocks)],
            near_send.at[k], near_recv.at[k], rows=partner,
        )

    def far(k):
        return remote(
            vecs.at[:, pl.ds(near_off + got(k), step_blocks)],
            vecs.at[:, pl.ds(far_off + got(k), step_blocks)],
            far_send.at[k], far_recv.at[k], rows=ahead,
        )

    def to_across(k):
        return remote(left_all.at[col, k], left_all.at[col, k], across_send.at[k], across_recv.at[k], cols=across)

    def to_mate(k):
        return remote(left_all.at[col, k], left_all.at[col, k], mate_send.at[k], mate_recv.at[k], cols=mate)

    def passed(k):
        return remote(left_all.at[across, k], left_all.at[across, k], pass_send.at[k], pass_recv.at[k], cols=mate)

    for k in range(CHUNKS):
        near(k).start()
    own_left.wait()
    for k in range(LEFT_CHUNKS):
        for c in range(2):
            left_all[col, k, c * width:(c + 1) * width, :] = left_own[c, k * step_rows:(k + 1) * step_rows, :].T
        to_across(k).start()
        to_mate(k).start()
    own_vecs.start()
    own_dip.start()

    def pair(at):
        real = vecs[0, at]
        imag = vecs[1, at]
        pairs[at, :size, :width] = real
        pairs[at, :size, width:] = imag
        pairs[at, size:, :width] = -imag
        pairs[at, size:, width:] = real

    def lay_out(i, carry):
        count = counts_ref[i]
        for j in range(slots):
            for c in range(2):
                block = dip[i, j, c]
                at = (2 * j + c) * size
                mats[i, :, at:at + size] = jnp.where(j < count, block, jnp.zeros_like(block))
        return carry

    def far_pairs(k):
        @pl.when(has_behind)
        def _():
            far(k).wait_recv()

        for b in range(step_blocks):
            pair(far_off + got(k) + b)

    lag = CHUNKS // 4
    half_way = CHUNKS // 2
    every = CHUNKS // LEFT_CHUNKS
    per_step = blocks // half_way
    for k in range(CHUNKS):
        near(k).wait_recv()

        @pl.when(has_ahead)
        def _():
            far(k).start()

        if k % every == every - 1:
            to_across(k // every).wait_recv()
            passed(k // every).start()
        for b in range(step_blocks):
            pair(near_off + got(k) + b)
        if k < half_way:
            if k == 0:
                own_vecs.wait()
            for b in range(per_step):
                pair(blocks + k * per_step + b)
        else:
            if k == half_way:
                own_dip.wait()
            start = (k - half_way) * per_step
            lax.fori_loop(start, start + per_step, lay_out, 0)
        if k >= lag:
            far_pairs(k - lag)
        if reduce_inside and k < n // 2:
            if k > 0:
                pl.semaphore_wait(round_sem.at[k - 1], neighbours)
            if k < n // 2 - 1:
                greet(round_sem.at[k])
    first = (me - 1) * blocks

    def block_row(at, carry):
        i = at * parity + (blocks - 1 - at) * (1 - parity)
        total = jnp.zeros((size, 2 * width), jnp.float32)
        for j in range(slots):
            source = jnp.clip(cols_ref[j, i] - first, 0, 3 * blocks - 1)
            lhs = mats[i, :, 2 * j * size:2 * (j + 1) * size]
            total = total + jnp.dot(lhs, pairs[source], preferred_element_type=jnp.float32)
        image[pl.ds(i * size, size), :] = total.astype(image.dtype)
        return carry

    ready = blocks - lag * step_blocks
    lax.fori_loop(0, ready, block_row, 0, unroll=4)
    for k in range(CHUNKS - lag, CHUNKS):
        far_pairs(k)
    lax.fori_loop(ready, blocks, block_row, 0, unroll=4)

    for k in range(LEFT_CHUNKS):
        to_mate(k).wait_recv()
        passed(k).wait_recv()

    def product(g):
        total = jnp.zeros((2 * width, 2 * width), jnp.float32)
        for k in range(LEFT_CHUNKS):
            total = total + jnp.dot(
                left_all[g, k], image[k * step_rows:(k + 1) * step_rows, :], preferred_element_type=jnp.float32
            )
        real_part = total[:width, :width] + total[width:, width:]
        imag_part = total[:width, width:] - total[width:, :width]
        return real_part, imag_part

    if not reduce_inside:
        for g in range(groups):
            real_part, imag_part = product(g)
            out_ref[g, 0] = real_part
            out_ref[g, 1] = imag_part
    else:
        share = width // n
        half = groups // HALVES
        order = sorted(range(1, n), key=lambda d: abs(d - n // 2))

        def give(h, d):
            peer = lax.rem(me + d, n)
            return remote(part.at[h, peer], landed.at[h, me], share_send.at[h, peer], share_recv.at[h, me], rows=peer)

        def take(h, d):
            peer = lax.rem(me + d, n)
            return remote(part.at[h, peer], landed.at[h, peer], share_send.at[h, peer], share_recv.at[h, peer], rows=peer)

        def spread(h, d):
            peer = lax.rem(col + d, groups)
            return remote(final.at[h, col], final.at[h, col], final_send.at[h, d], final_recv.at[h, col], cols=peer)

        def gather(h, d):
            peer = lax.rem(col + d, groups)
            return remote(final.at[h, peer], final.at[h, peer], final_send.at[h, d], final_recv.at[h, peer], cols=peer)

        for h in range(HALVES):
            for g in range(half):
                real_part, imag_part = product(h * half + g)
                part[h, :, g, 0] = real_part.astype(part.dtype).reshape(n, share, width)
                part[h, :, g, 1] = imag_part.astype(part.dtype).reshape(n, share, width)
            for d in order:
                give(h, d).start()
        for h in range(HALVES):
            total = part[h, me].astype(jnp.float32)
            for d in order[::-1]:
                take(h, d).wait_recv()
                total = total + landed[h, lax.rem(me + d, n)].astype(jnp.float32)
            final[h, col] = total
            for d in (2, 3, 1):
                spread(h, d).start()
        for h in range(HALVES):
            for d in range(1, groups):
                gather(h, d).wait_recv()
            for c in range(groups):
                for part_at in range(2):
                    out_ref[h * half:(h + 1) * half, :, part_at, c * width:(c + 1) * width] = final[h, c, :, part_at]
        for h in range(HALVES):
            for d in order:
                give(h, d).wait_send()
            for d in range(1, groups):
                spread(h, d).wait_send()

    for k in range(CHUNKS):
        near(k).wait_send()

        @pl.when(has_ahead)
        def _():
            far(k).wait_send()

    for k in range(LEFT_CHUNKS):
        to_across(k).wait_send()
        to_mate(k).wait_send()
        passed(k).wait_send()


def local(n, groups, right_vecs, left_vecs, dip_blocks, block_cols, block_counts):
    span, width = right_vecs.shape[1:]
    blocks, slots, _, size, _ = dip_blocks.shape
    share = width // n
    reduce_inside = share % 16 == 0
    right = right_vecs.reshape(2, blocks, size, width)
    if reduce_inside:
        half = groups // HALVES
        out_shape = (groups, share, 2, groups * width)
        part_shape = (HALVES, n, half, 2, share, width)
        final_shape = (HALVES, groups, half, 2, share, width)
    else:
        out_shape = (groups, 2, width, width)
        part_shape = final_shape = (1, 1, 1, 16, 128)
    dma = pltpu.SemaphoreType.DMA
    result = pl.pallas_call(
        functools.partial(kernel, n, groups, reduce_inside),
        out_shape=jax.ShapeDtypeStruct(out_shape, jnp.float32),
        in_specs=[pl.BlockSpec(memory_space=pltpu.SMEM)] * 2 + [pl.BlockSpec(memory_space=pl.ANY)] * 3,
        out_specs=pl.BlockSpec(memory_space=pltpu.VMEM),
        scratch_shapes=[
            pltpu.VMEM((2, 3 * blocks, size, width), jnp.bfloat16),
            pltpu.VMEM((2, span, width), jnp.bfloat16),
            pltpu.VMEM((groups, LEFT_CHUNKS, 2 * width, span // LEFT_CHUNKS), jnp.bfloat16),
            pltpu.VMEM(dip_blocks.shape, jnp.bfloat16),
            pltpu.VMEM((3 * blocks, 2 * size, 2 * width), jnp.bfloat16),
            pltpu.VMEM((blocks, size, 2 * slots * size), jnp.bfloat16),
            pltpu.VMEM((span, 2 * width), jnp.bfloat16),
            pltpu.VMEM(part_shape, jnp.bfloat16),
            pltpu.VMEM(part_shape, jnp.bfloat16),
            pltpu.VMEM(final_shape, jnp.float32),
        ] + [dma((CHUNKS,))] * 4 + [dma((LEFT_CHUNKS,))] * 6 + [
            dma((2,)), dma, dma((HALVES, n)), dma((HALVES, n)), dma((HALVES, groups)), dma((HALVES, groups)),
            pltpu.SemaphoreType.REGULAR((max(n // 2 - 1, 1),)),
        ],
        compiler_params=pltpu.CompilerParams(
            collective_id=0, has_side_effects=True, vmem_limit_bytes=60 * 1024 * 1024
        ),
    )(block_cols.T, block_counts, right, left_vecs, dip_blocks)
    if reduce_inside:
        return result
    shares = lax.psum_scatter(jnp.transpose(result, (0, 2, 1, 3)), "rows", scatter_dimension=1, tiled=True)
    return lax.all_gather(shares, "cols", axis=3, tiled=True)


def solution(mesh):
    in_specs = (
        P(None, "rows", "cols"),
        P(None, "rows", "cols"),
        P("rows", None, None, None, None),
        P("rows", None),
        P("rows"),
    )
    out_specs = P(None, "rows", None, None)
    body = functools.partial(local, mesh.shape["rows"], mesh.shape["cols"])
    return jax.shard_map(body, mesh=mesh, in_specs=in_specs, out_specs=out_specs, check_vma=False)
```
